32 devices in a mesh: col: 16 (over z, y, core), row: 2 (over x).
Axes of the slice: x: 2, y: 2, z: 4, core: 2. Of those that a mesh axis runs over, the one named last changes fastest.
Arguments:
- anc_inverse: bfloat16 [4096, 4096], P('col', 'row'), may hold values from -6 to 6
- factor_rows: bfloat16 [16, 256, 2048], P('col', None, 'row'), may hold values from -0.09375 to 0.09375
- structure: int32 [8, 12], replicated, may hold values from 0 to 15, all different within a row
- pivot_inverse: float32 [8, 256, 256], P('row'), may hold values from -6 to 6
Outputs:
- selected: bfloat16 [16, 256, 2048], P('col', None, 'row')
- diagonal_blocks: float32 [8, 256, 256], P('row')
The draws below stay inside these ranges and needn't reach their ends.
Inputs may be any that keep to these rules, and one draw needn't show every extreme that they name: `structure`: each row names 12 different ancestors; every ancestor is named by some row.
All inputs are finite; a program needn't handle non-finite values.
Results may differ from the reference program's by a relative error of at most 0.0016.
Values may be sent and summed in bfloat16 or wider, within the bound.
No kernel may reach another device: no remote copies, remote signals or barrier semaphores. Data moves between devices by JAX's collectives and lax.ppermute only.
A program may use at most 64 MiB of HBM per device.

```python
import jax
import jax.numpy as jnp
from jax import lax

B = 256
NLEV = 8
AS = 16
NSTR = 12
NA = 4096
NL = 2048


def block_scale(key, shape, cuts, low, high):
    loudness = 1.0
    for dim, parts in cuts:
        heights = jax.random.uniform(jax.random.fold_in(jax.random.fold_in(key, 6), dim), (parts,), jnp.float32, low / len(cuts), high / len(cuts))
        loudness = loudness * jnp.repeat(jnp.exp(heights), shape[dim] // parts).reshape((-1,) + (1,) * (len(shape) - 1 - dim))
    return loudness


def distinct(rng, rows, number_of, top, lift):
    ranking = jax.random.permutation(jax.random.fold_in(rng, 1), number_of)
    pull = ranking
    for power in range(3):
        pull = pull * pull // number_of
    pull = pull * lift // number_of
    tickets = jax.random.randint(jax.random.fold_in(rng, 2), (rows, number_of), 0, 4096) + pull
    fixed_rows = jax.random.permutation(jax.random.fold_in(rng, 3), rows)[jnp.arange(number_of) % rows]
    tickets = jnp.where(jnp.arange(rows)[:, None] == fixed_rows[None, :], 1 << 14, tickets)
    score = tickets * number_of + jnp.arange(number_of)
    return lax.top_k(score.astype(jnp.int32), top)[1].astype(jnp.int32)


def noise(stream_key, extent, deviation, limit, cuts=(), kind=jnp.bfloat16):
    values = deviation * jax.random.normal(stream_key, extent, jnp.float32)
    if cuts:
        values = values * block_scale(stream_key, extent, cuts, -0.22, 0.18)
    return jnp.clip(values, -limit, limit).astype(kind)


def setup_inputs(seed: int = 0) -> dict:
    keys = jax.random.split(jax.random.key(seed), 5)
    anc_inverse = noise(keys[0], (NA, B * AS), 1.0, 6.0, ((0, 16), (1, 2)))
    factor_rows = noise(keys[1], (AS, B, NL), NA ** -0.5, 0.09375, ((0, 16), (2, 2)))
    structure = distinct(keys[2], NLEV, AS, NSTR, 6144)
    pivot_inverse = noise(keys[3], (NLEV, B, B), 1.0, 6.0, ((0, 2),), jnp.float32)
    return dict(anc_inverse=anc_inverse, factor_rows=factor_rows, structure=structure, pivot_inverse=pivot_inverse)


def reference(anc_inverse, factor_rows, structure, pivot_inverse):
    member = jnp.any(structure[:, :, None] == jnp.arange(AS, dtype=jnp.int32)[None, None, :], axis=1)
    keep_mask = jnp.repeat(member.T, B, axis=1)
    masked = jnp.where(keep_mask[:, None, :], factor_rows, jnp.zeros_like(factor_rows))
    inverse = anc_inverse.astype(jnp.float32).reshape(NA, B, AS).transpose(0, 2, 1).reshape(NA, NA)
    product = jnp.dot(inverse, masked.astype(jnp.float32).reshape(NA, NL), precision=lax.Precision.HIGHEST, preferred_element_type=jnp.float32)
    selected = jnp.where(keep_mask[:, None, :], -product.reshape(AS, B, NL), jnp.zeros((AS, B, NL), jnp.float32)).astype(jnp.bfloat16)
    factor_flat = masked.astype(jnp.float32).reshape(NA, NLEV, B)
    selected_flat = selected.astype(jnp.float32).reshape(NA, NLEV, B)
    diagonal_blocks = pivot_inverse - jnp.einsum("ikp,ikq->kpq", factor_flat, selected_flat, precision=lax.Precision.HIGHEST)
    return selected, diagonal_blocks
```

```python
import functools

import jax
import jax.numpy as jnp
from jax import lax
from jax.experimental import pallas as pl
from jax.experimental.pallas import tpu as pltpu
from jax.sharding import PartitionSpec as P

VMEM = pl.BlockSpec(memory_space=pltpu.VMEM)
SMEM = pl.BlockSpec(memory_space=pltpu.SMEM)
PARAMS = pltpu.CompilerParams(vmem_limit_bytes=40 * 1024 * 1024)
GROUP = 4


def generic(anc_inverse, factor_rows, structure, pivot_inverse):
    own_blocks = factor_rows.shape[0]
    width = factor_rows.shape[1]
    local_cols = factor_rows.shape[2]
    local_sups = local_cols // width
    inv_rows = anc_inverse.shape[0]
    all_blocks = own_blocks * lax.axis_size("col")
    col_index = lax.axis_index("col")
    row_index = lax.axis_index("row")
    blocks = col_index * own_blocks + jnp.arange(own_blocks, dtype=jnp.int32)
    list_rows = lax.dynamic_slice_in_dim(structure, row_index * local_sups, local_sups, 0)
    in_struct = jnp.any(list_rows[:, :, None] == blocks[None, None, :], axis=1)
    keep_bf = in_struct.T.astype(jnp.bfloat16)[:, None, :, None]
    keep_float = in_struct.T.astype(jnp.float32)[:, None, :, None]
    masked = (factor_rows.reshape(own_blocks, width, local_sups, width) * keep_bf).reshape(
        factor_rows.shape
    )
    gathered = lax.all_gather(anc_inverse, "row", axis=1, tiled=True)
    full_inverse = gathered.reshape(inv_rows, width, all_blocks)
    product = jnp.einsum(
        "iwb,bwn->in",
        full_inverse,
        lax.all_gather(masked, "col", axis=0, tiled=True),
        preferred_element_type=jnp.float32,
    )
    selected = (-(product.reshape(own_blocks, width, local_sups, width) * keep_float)).astype(
        jnp.bfloat16
    )
    selected = selected.reshape(factor_rows.shape)
    factor_flat = masked.reshape(own_blocks * width, local_sups, width)
    selected_flat = selected.reshape(own_blocks * width, local_sups, width)
    local_terms = jnp.einsum(
        "ikp,ikq->kpq", factor_flat, selected_flat, preferred_element_type=jnp.float32
    )
    summed = lax.psum(local_terms, "col")
    return (selected, pivot_inverse - summed)


def is_member(lists, sup, block):
    found = lists[sup, 0] == block
    for i in range(1, lists.shape[1]):
        found = jnp.logical_or(found, lists[sup, i] == block)
    return found


def split_kernel(place, lists, rows_ref, keep_ref, give_ref):
    col, row = place[0], place[1]
    width = rows_ref.shape[0]
    for j in range(GROUP):
        sup = (col % GROUP) ^ j
        part = rows_ref[:, pl.ds(pl.multiple_of(sup * width, width), width)]
        part = jnp.where(is_member(lists, row * GROUP + sup, col), part, jnp.zeros_like(part))
        (keep_ref if j % 2 == 0 else give_ref)[j // 2] = part


def product_kernel(n_groups, first, last, place, lists, *refs):
    m_refs, refs = refs[:10], refs[10:]
    a_refs, refs = refs[: 4 * n_groups], refs[4 * n_groups :]
    if last:
        before_ref, refs = refs[0], refs[1:]
    sel_ref, diag_ref = refs
    col, row = place[0], place[1]
    width = sel_ref.shape[1]
    half = width // 2
    near, far = pl.multiple_of(row * half, half), pl.multiple_of((1 - row) * half, half)

    def level(j, at):
        z, part = j // 4, (j // 2) % 2
        ref = m_refs[5 * part + z]
        block = ref[j % 2, pl.ds(at, half), :]
        if z == 3:
            block = block + m_refs[5 * part + 4][j % 2, pl.ds(at, half), :]
        return block

    sup = row * GROUP + col % GROUP
    diag = before_ref[...] if last else None
    totals = [None] * n_groups
    n_half = a_refs[0].shape[0]
    for j in range(16):
        m = jnp.concatenate([level(j, near), level(j, far)], axis=0)
        block = col ^ j
        in_low = block < n_half
        at = block % n_half
        for g in range(n_groups):
            low_near, high_near, low_far, high_far = a_refs[4 * g : 4 * g + 4]
            a_near = jnp.where(in_low, low_near[at], high_near[at])
            a_far = jnp.where(in_low, low_far[at], high_far[at])
            a = jnp.concatenate([a_near, a_far], axis=1)
            term = jnp.dot(a, m, preferred_element_type=jnp.float32)
            totals[g] = term if totals[g] is None else totals[g] + term
    for g in range(n_groups):
        kept = is_member(lists, sup, col ^ (first + g))
        sel = jnp.where(kept, -totals[g], jnp.zeros_like(totals[g])).astype(jnp.bfloat16)
        sel_ref[g] = sel
        left = m_refs[5 * ((first + g) // 2)][(first + g) % 2]
        term = lax.dot_general(
            left, sel, (((0,), (0,)), ((), ())), preferred_element_type=jnp.float32
        )
        diag = term if diag is None else diag + term
    diag_ref[...] = diag


def merge_kernel(place, own_ref, core_ref, pair_ref, cross_ref, out_ref):
    col = place[0]
    width = own_ref.shape[0]
    for j, ref in enumerate((own_ref, core_ref, pair_ref, cross_ref)):
        sup = (col % GROUP) ^ j
        out_ref[:, pl.ds(pl.multiple_of(sup * width, width), width)] = ref[...]


def finish_kernel(place, own_ref, other_ref, pivot_ref, out_ref):
    col = place[0]
    for j in range(GROUP):
        sup = (col % GROUP) ^ j
        ref = own_ref if j % 2 == 0 else other_ref
        out_ref[sup] = pivot_ref[sup] - ref[j // 2]


def per_device(anc_inverse, factor_rows, structure, pivot_inverse):
    width = factor_rows.shape[1]
    n_col = lax.axis_size("col")
    all_blocks = factor_rows.shape[0] * n_col
    bf16, f32 = jnp.bfloat16, jnp.float32
    col = lax.axis_index("col")
    row = lax.axis_index("row")
    place = jnp.stack([col, row]).astype(jnp.int32)
    rows = anc_inverse.shape[0]
    half_w = anc_inverse.shape[1] // all_blocks

    def swap(x, flip):
        return lax.ppermute(x, "col", [(c, c ^ flip) for c in range(n_col)])

    def middle(x):
        return lax.ppermute(x, "col", [(c, c ^ 12) for c in range(n_col) if c // 4 in (1, 2)])

    def outward(x):
        return lax.ppermute(x, "col", [(c, c ^ 4) for c in range(n_col) if c // 4 in (1, 2)])

    def across(x):
        return lax.ppermute(x, "row", [(0, 1), (1, 0)])

    cut = jax.ShapeDtypeStruct((2, width, width), bf16)
    keep, give = pl.pallas_call(
        split_kernel,
        out_shape=(cut, cut),
        in_specs=[SMEM, SMEM, VMEM],
        out_specs=(VMEM, VMEM),
        compiler_params=PARAMS,
    )(place, structure, factor_rows.reshape(width, -1))
    got = swap(give, 1)
    part_a = jnp.stack([keep[0], got[0]])
    part_b = swap(jnp.stack([keep[1], got[1]]), 2)
    level = []
    for part in (part_a, part_b):
        two = swap(part, 8)
        one = swap(part, 4)
        level += [part, one, two, middle(part), outward(two)]

    inverse = anc_inverse.reshape(rows, half_w, all_blocks).transpose(2, 0, 1)
    low, high = inverse[: all_blocks // 2], inverse[all_blocks // 2 :]
    x_low, x_high = across(low), across(high)
    y_high, y_low = swap(high, 2), swap(low, 2)
    xy_low, xy_high = swap(x_low, 2), across(y_high)
    near = [low, high, x_low, x_high]
    far = [y_low, y_high, xy_low, xy_high]
    near += [swap(v, 1) for v in near]
    far += [swap(v, 1) for v in far]

    sel_shape = jax.ShapeDtypeStruct((2, width, width), bf16)
    diag_shape = jax.ShapeDtypeStruct((width, width), f32)

    def product(first, last, groups, *extra):
        return pl.pallas_call(
            functools.partial(product_kernel, 2, first, last),
            out_shape=(sel_shape, diag_shape),
            in_specs=[SMEM, SMEM] + [VMEM] * (18 + len(extra)),
            out_specs=(VMEM, VMEM),
            compiler_params=PARAMS,
        )(place, structure, *level, *groups, *extra)

    sel_near, diag = product(0, False, near)
    sel_far, diag = product(2, True, far, diag)

    diag = diag + swap(diag, 4)
    diag = diag + swap(diag, 8)
    pair = jnp.stack([diag, swap(diag, 2)])
    other = swap(pair, 1)
    diagonal = pl.pallas_call(
        finish_kernel,
        out_shape=jax.ShapeDtypeStruct(pivot_inverse.shape, f32),
        in_specs=[SMEM, VMEM, VMEM, VMEM],
        out_specs=VMEM,
        compiler_params=PARAMS,
    )(place, pair, other, pivot_inverse)

    selected = pl.pallas_call(
        merge_kernel,
        out_shape=jax.ShapeDtypeStruct((width, GROUP * width), bf16),
        in_specs=[SMEM, VMEM, VMEM, VMEM, VMEM],
        out_specs=VMEM,
        compiler_params=PARAMS,
    )(place, sel_near[0], swap(sel_near[1], 1), swap(sel_far[0], 2), swap(sel_far[1], 3))
    return selected.reshape(factor_rows.shape), diagonal


def solution(mesh):
    in_specs = (P("col", "row"), P("col", None, "row"), P(), P("row", None, None))
    out_specs = (P("col", None, "row"), P("row", None, None))

    def run(anc_inverse, factor_rows, structure, pivot_inverse):
        n_col, n_row = mesh.shape["col"], mesh.shape["row"]
        blocks, width, columns = factor_rows.shape
        fits = n_col == 16 and n_row == 2 and blocks == n_col and columns == n_row * GROUP * width
        return jax.shard_map(
            per_device if fits else generic,
            mesh=mesh,
            in_specs=in_specs,
            out_specs=out_specs,
            check_vma=False,
        )(anc_inverse, factor_rows, structure, pivot_inverse)

    return run
```

```python
import functools

import jax
import jax.numpy as jnp
from jax import lax
from jax.experimental import pallas as pl
from jax.experimental.pallas import tpu as pltpu
from jax.sharding import PartitionSpec as P

VMEM = pl.BlockSpec(memory_space=pltpu.VMEM)
SMEM = pl.BlockSpec(memory_space=pltpu.SMEM)
PARAMS = pltpu.CompilerParams(vmem_limit_bytes=40 * 1024 * 1024)
GROUP = 4


def after(x, *earlier):
    return lax.optimization_barrier((x, *earlier))[0]


def together(wanted, *earlier):
    return lax.optimization_barrier((*wanted, *earlier))[: len(wanted)]


def generic(anc_inverse, factor_rows, structure, pivot_inverse):
    own_blocks = factor_rows.shape[0]
    width = factor_rows.shape[1]
    local_cols = factor_rows.shape[2]
    local_sups = local_cols // width
    inv_rows = anc_inverse.shape[0]
    all_blocks = own_blocks * lax.axis_size("col")
    col_index = lax.axis_index("col")
    row_index = lax.axis_index("row")
    blocks = col_index * own_blocks + jnp.arange(own_blocks, dtype=jnp.int32)
    list_rows = lax.dynamic_slice_in_dim(structure, row_index * local_sups, local_sups, 0)
    in_struct = jnp.any(list_rows[:, :, None] == blocks[None, None, :], axis=1)
    keep_bf = in_struct.T.astype(jnp.bfloat16)[:, None, :, None]
    keep_float = in_struct.T.astype(jnp.float32)[:, None, :, None]
    masked = (factor_rows.reshape(own_blocks, width, local_sups, width) * keep_bf).reshape(
        factor_rows.shape
    )
    gathered = lax.all_gather(anc_inverse, "row", axis=1, tiled=True)
    full_inverse = gathered.reshape(inv_rows, width, all_blocks)
    product = jnp.einsum(
        "iwb,bwn->in",
        full_inverse,
        lax.all_gather(masked, "col", axis=0, tiled=True),
        preferred_element_type=jnp.float32,
    )
    selected = (-(product.reshape(own_blocks, width, local_sups, width) * keep_float)).astype(
        jnp.bfloat16
    )
    selected = selected.reshape(factor_rows.shape)
    factor_flat = masked.reshape(own_blocks * width, local_sups, width)
    selected_flat = selected.reshape(own_blocks * width, local_sups, width)
    local_terms = jnp.einsum(
        "ikp,ikq->kpq", factor_flat, selected_flat, preferred_element_type=jnp.float32
    )
    summed = lax.psum(local_terms, "col")
    return (selected, pivot_inverse - summed)


def is_member(lists, sup, block):
    found = lists[sup, 0] == block
    for i in range(1, lists.shape[1]):
        found = jnp.logical_or(found, lists[sup, i] == block)
    return found


def split_kernel(place, lists, rows_ref, keep_ref, give_ref):
    col, row = place[0], place[1]
    width = rows_ref.shape[0]
    for j in range(GROUP):
        sup = (col % GROUP) ^ j
        part = rows_ref[:, pl.ds(pl.multiple_of(sup * width, width), width)]
        part = jnp.where(is_member(lists, row * GROUP + sup, col), part, jnp.zeros_like(part))
        (keep_ref if j % 2 == 0 else give_ref)[j // 2] = part


def product_kernel(segments, first, place, lists, *refs):
    own, one_a, one_b, two_a, two_b, three, out_a, out_b = refs[:8]
    n_inverse = 1 + max(at[0] for group in segments for side in group for at in side)
    inverse, refs = refs[8 : 8 + n_inverse], refs[8 + n_inverse :]
    if first:
        before_ref, refs = refs[0], refs[1:]
    sel_ref, diag_ref, level = refs
    col, row = place[0], place[1]
    n_blocks, width = level.shape[0], level.shape[1]
    half = width // 2
    one, two, out = (one_a, one_b), (two_a, two_b), (out_a, out_b)
    for j in range(n_blocks):
        z, i = j // GROUP, j % GROUP
        for side in range(2):
            rows = pl.ds(pl.multiple_of((row if side == 0 else 1 - row) * half, half), half)
            if z == 0:
                part = own[i, rows, :]
            elif z == 1:
                part = one[i // 2][i % 2, rows, :]
            elif z == 2:
                part = two[i // 2][i % 2, rows, :]
            else:
                part = three[i, rows, :] + out[i // 2][i % 2, rows, :]
            level[col ^ j, side * half : (side + 1) * half] = part

    sup = row * GROUP + col % GROUP
    diag = before_ref[...] if first else None
    for g, group in enumerate(segments):
        total = None
        for block in range(n_blocks):
            (near, i), (far, k) = group[0][block], group[1][block]
            a = jnp.concatenate([inverse[near][i], inverse[far][k]], axis=1)
            term = jnp.dot(a, level[block], preferred_element_type=jnp.float32)
            total = term if total is None else total + term
        kept = is_member(lists, sup, col ^ (first + g))
        sel = jnp.where(kept, -total, jnp.zeros_like(total)).astype(jnp.bfloat16)
        sel_ref[g] = sel
        term = lax.dot_general(
            own[first + g], sel, (((0,), (0,)), ((), ())), preferred_element_type=jnp.float32
        )
        diag = term if diag is None else diag + term
    diag_ref[...] = diag


def merge_kernel(place, own_ref, core_ref, pair_ref, cross_ref, out_ref):
    col = place[0]
    width = own_ref.shape[0]
    for j, ref in enumerate((own_ref, core_ref, pair_ref, cross_ref)):
        sup = (col % GROUP) ^ j
        out_ref[:, pl.ds(pl.multiple_of(sup * width, width), width)] = ref[...]


def finish_kernel(place, own_ref, other_ref, pivot_ref, out_ref):
    col = place[0]
    for j in range(GROUP):
        sup = (col % GROUP) ^ j
        ref = own_ref if j % 2 == 0 else other_ref
        out_ref[sup] = pivot_ref[sup] - ref[j // 2]


def per_device(anc_inverse, factor_rows, structure, pivot_inverse):
    width = factor_rows.shape[1]
    n_col = lax.axis_size("col")
    all_blocks = factor_rows.shape[0] * n_col
    bf16, f32 = jnp.bfloat16, jnp.float32
    col = lax.axis_index("col")
    row = lax.axis_index("row")
    place = jnp.stack([col, row]).astype(jnp.int32)
    rows = anc_inverse.shape[0]
    half_w = anc_inverse.shape[1] // all_blocks

    def swap(x, flip):
        return lax.ppermute(x, "col", [(c, c ^ flip) for c in range(n_col)])

    def middle(x):
        return lax.ppermute(x, "col", [(c, c ^ 12) for c in range(n_col) if c // 4 in (1, 2)])

    def outward(x):
        return lax.ppermute(x, "col", [(c, c ^ 4) for c in range(n_col) if c // 4 in (1, 2)])

    def across(x):
        return lax.ppermute(x, "row", [(0, 1), (1, 0)])

    turned = anc_inverse.T
    cut = jax.ShapeDtypeStruct((2, width, width), bf16)
    keep, give = pl.pallas_call(
        split_kernel,
        out_shape=(cut, cut),
        in_specs=[SMEM, SMEM, VMEM],
        out_specs=(VMEM, VMEM),
        compiler_params=PARAMS,
    )(place, structure, after(factor_rows.reshape(width, -1), turned))
    got = swap(give, 1)
    inverse = turned.reshape(half_w, all_blocks, rows).transpose(1, 2, 0)
    x1, y1, y2 = all_blocks // 2, 4 * all_blocks // 16, 14 * all_blocks // 16

    part_a = jnp.stack([keep[0], got[0]])
    for_pair = jnp.stack([keep[1], got[1]])
    first = together((part_a, for_pair, inverse[:x1], inverse[:y1]))
    two_a, one_a = swap(first[0], 8), swap(first[0], 4)
    part_b, x_a, y_a = swap(first[1], 2), across(first[2]), swap(first[3], 2)

    second = together((part_b, two_a, inverse[x1:], inverse[y1:y2], inverse, x_a, y_a), one_a)
    two_b, out_a = swap(second[0], 8), outward(second[1])
    x_b, y_b = across(second[2]), swap(second[3], 2)
    c_own = swap(second[4], 1)

    own = jnp.concatenate([part_a, part_b])
    mixed = jnp.concatenate([inverse[y2:], x_a[:y1], x_b[y2 - x1 :]])
    third = together((two_b, own, y_b, mixed, part_b), out_a, c_own, x_b)
    out_b, three, one_b = outward(third[0]), middle(third[1]), swap(third[4], 4)
    xy_mid, y_mixed = across(third[2]), swap(third[3], 2)
    cores = together((x_a, x_b, y_a, y_b), one_b, out_b)
    cx_a, cx_b, cy_a, cy_b = (swap(v, 1) for v in cores)

    last = together((xy_mid, y_mixed), three)
    cxy_mid, cy_mixed = swap(last[0], 1), swap(last[1], 1)

    level = [own, one_a, one_b, two_a, two_b, three, out_a, out_b]
    blocks = range(all_blocks)
    whole = [(0, b) for b in blocks]

    def halves(k):
        return [(k, b) if b < x1 else (k + 1, b - x1) for b in blocks]

    def pair_rows(k):
        return [(k, b) if b < y1 else (k + 1, b - y1) if b < y2 else (k + 2, b - y2) for b in blocks]

    def cross_rows(k, m):
        tail = all_blocks - y2
        return [
            (m, b - y1) if y1 <= b < y2 else (k, tail + (b if b < y1 else b - y2 + y1)) for b in blocks
        ]

    def other(at, k):
        return [(which + k, i) for which, i in at]

    near = [inverse, x_a, x_b, c_own, cx_a, cx_b]
    near_at = [[whole, halves(1)], [other(whole, 3), halves(4)]]
    far = [y_a, y_b, y_mixed, xy_mid, cy_a, cy_b, cy_mixed, cxy_mid]
    far_at = [[pair_rows(0), cross_rows(2, 3)], [pair_rows(4), cross_rows(6, 7)]]

    def product(first, at, *arrays):
        return pl.pallas_call(
            functools.partial(product_kernel, at, first),
            out_shape=(
                jax.ShapeDtypeStruct((2, width, width), bf16),
                jax.ShapeDtypeStruct((width, width), f32),
            ),
            in_specs=[SMEM, SMEM] + [VMEM] * (len(level) + len(arrays)),
            out_specs=(VMEM, VMEM),
            scratch_shapes=[pltpu.VMEM((all_blocks, width, width), bf16)],
            compiler_params=PARAMS,
        )(place, structure, *level, *arrays)

    sel_near, diag = product(0, near_at, *near)
    s_core = swap(sel_near[1], 1)
    sel_far, diag = product(2, far_at, *far, diag)
    s_pair, s_cross = swap(sel_far[0], 2), swap(sel_far[1], 3)

    diag = diag + swap(diag, 4)
    diag = diag + swap(after(diag, s_core, s_pair, s_cross), 8)
    selected = pl.pallas_call(
        merge_kernel,
        out_shape=jax.ShapeDtypeStruct((width, GROUP * width), bf16),
        in_specs=[SMEM, VMEM, VMEM, VMEM, VMEM],
        out_specs=VMEM,
        compiler_params=PARAMS,
    )(place, sel_near[0], s_core, s_pair, s_cross)
    pair = jnp.stack([diag, swap(after(diag, selected), 2)])
    other = swap(pair, 1)
    diagonal = pl.pallas_call(
        finish_kernel,
        out_shape=jax.ShapeDtypeStruct(pivot_inverse.shape, f32),
        in_specs=[SMEM, VMEM, VMEM, VMEM],
        out_specs=VMEM,
        compiler_params=PARAMS,
    )(place, pair, other, pivot_inverse)
    return selected.reshape(factor_rows.shape), diagonal


def solution(mesh):
    in_specs = (P("col", "row"), P("col", None, "row"), P(), P("row", None, None))
    out_specs = (P("col", None, "row"), P("row", None, None))

    def run(anc_inverse, factor_rows, structure, pivot_inverse):
        n_col, n_row = mesh.shape["col"], mesh.shape["row"]
        blocks, width, columns = factor_rows.shape
        fits = n_col == 16 and n_row == 2 and blocks == n_col and columns == n_row * GROUP * width
        return jax.shard_map(
            per_device if fits else generic,
            mesh=mesh,
            in_specs=in_specs,
            out_specs=out_specs,
            check_vma=False,
        )(anc_inverse, factor_rows, structure, pivot_inverse)

    return run
```

```python
import functools

import jax
import jax.numpy as jnp
from jax import lax
from jax.experimental import pallas as pl
from jax.experimental.pallas import tpu as pltpu
from jax.sharding import PartitionSpec as P

VMEM = pl.BlockSpec(memory_space=pltpu.VMEM)
SMEM = pl.BlockSpec(memory_space=pltpu.SMEM)
PARAMS = pltpu.CompilerParams(vmem_limit_bytes=24 * 1024 * 1024)
TOP = 14.0
GROUP = 4


def after(x, *earlier):
    return lax.optimization_barrier((x, *earlier))[0]


def together(wanted, *earlier):
    return lax.optimization_barrier((*wanted, *earlier))[: len(wanted)]


def generic(anc_inverse, factor_rows, structure, pivot_inverse):
    own_blocks = factor_rows.shape[0]
    width = factor_rows.shape[1]
    local_cols = factor_rows.shape[2]
    local_sups = local_cols // width
    inv_rows = anc_inverse.shape[0]
    all_blocks = own_blocks * lax.axis_size("col")
    col_index = lax.axis_index("col")
    row_index = lax.axis_index("row")
    blocks = col_index * own_blocks + jnp.arange(own_blocks, dtype=jnp.int32)
    list_rows = lax.dynamic_slice_in_dim(structure, row_index * local_sups, local_sups, 0)
    in_struct = jnp.any(list_rows[:, :, None] == blocks[None, None, :], axis=1)
    keep_bf = in_struct.T.astype(jnp.bfloat16)[:, None, :, None]
    keep_float = in_struct.T.astype(jnp.float32)[:, None, :, None]
    masked = (factor_rows.reshape(own_blocks, width, local_sups, width) * keep_bf).reshape(
        factor_rows.shape
    )
    gathered = lax.all_gather(anc_inverse, "row", axis=1, tiled=True)
    full_inverse = gathered.reshape(inv_rows, width, all_blocks)
    product = jnp.einsum(
        "iwb,bwn->in",
        full_inverse,
        lax.all_gather(masked, "col", axis=0, tiled=True),
        preferred_element_type=jnp.float32,
    )
    selected = (-(product.reshape(own_blocks, width, local_sups, width) * keep_float)).astype(
        jnp.bfloat16
    )
    selected = selected.reshape(factor_rows.shape)
    factor_flat = masked.reshape(own_blocks * width, local_sups, width)
    selected_flat = selected.reshape(own_blocks * width, local_sups, width)
    local_terms = jnp.einsum(
        "ikp,ikq->kpq", factor_flat, selected_flat, preferred_element_type=jnp.float32
    )
    summed = lax.psum(local_terms, "col")
    return (selected, pivot_inverse - summed)


def is_member(lists, sup, block):
    found = lists[sup, 0] == block
    for i in range(1, lists.shape[1]):
        found = jnp.logical_or(found, lists[sup, i] == block)
    return found


def product_kernel(slots, n_level, groups, begins, ends, packs, place, lists, *refs):
    level, refs = refs[:n_level], refs[n_level:]
    sides, refs = refs[: 2 * len(groups)], refs[2 * len(groups) :]
    n_extra = 1 if groups[0] >= 2 else 0
    highs, refs = refs[: n_extra * len(groups)], refs[n_extra * len(groups) :]
    if not begins:
        sums_ref, refs = refs[0], refs[1:]
    if packs:
        before_ref, refs = refs[0], refs[1:]
    col, row = place[0], place[1]
    width = level[0].shape[1]
    half = width // 2
    sup = row * GROUP + col % GROUP
    near = pl.ds(pl.multiple_of(row * half, half), half)
    far = pl.ds(pl.multiple_of((1 - row) * half, half), half)
    totals = [None if begins else sums_ref[g] for g in range(len(groups))]
    for slot in slots:
        z, i = slot // GROUP, slot % GROUP
        block = col ^ slot
        parts = [level[z][i, rows, :] for rows in (near, far)]
        if z == 3:
            parts = [part + level[4][i, rows, :] for part, rows in zip(parts, (near, far))]
        m = jnp.concatenate(parts, axis=0)
        m = jnp.where(is_member(lists, sup, block), m, jnp.zeros_like(m))
        for g in range(len(groups)):
            a_near = sides[2 * g][block]
            if n_extra:
                low, high = sides[2 * g + 1], highs[g]
                n_low = low.shape[0]
                in_low = block < n_low
                a_far = jnp.where(
                    in_low, low[jnp.minimum(block, n_low - 1)], high[jnp.maximum(block - n_low, 0)]
                )
            else:
                a_far = sides[2 * g + 1][block]
            a = jnp.concatenate([a_near, a_far], axis=1)
            term = jnp.dot(a, m, preferred_element_type=jnp.float32)
            totals[g] = term if totals[g] is None else totals[g] + term
    if not ends:
        for g in range(len(groups)):
            refs[0][g] = totals[g]
        return
    sel_ref, diag_ref = refs
    diag = before_ref[...] if packs else None
    for g, group in enumerate(groups):
        kept = is_member(lists, sup, col ^ group)
        sel = jnp.where(kept, -totals[g], jnp.zeros_like(totals[g])).astype(jnp.bfloat16)
        sel_ref[g] = sel
        term = lax.dot_general(
            level[0][group], sel, (((0,), (0,)), ((), ())), preferred_element_type=jnp.float32
        )
        diag = term if diag is None else diag + term
    if not packs:
        diag_ref[...] = diag
        return
    largest = jnp.maximum(jnp.max(jnp.abs(diag)), 1e-30)
    power = jnp.ceil(jnp.log2(jnp.full((8, 128), largest, jnp.float32)))
    power = jnp.concatenate([power] * (width // 128), axis=1)
    diag_ref[:width] = diag * jnp.exp2(TOP - power[:1])
    for at in range(width, diag_ref.shape[0], 8):
        diag_ref[at : at + 8] = power


def merge_kernel(place, own_ref, core_ref, pair_ref, cross_ref, out_ref):
    col = place[0]
    width = own_ref.shape[0]
    for j, ref in enumerate((own_ref, core_ref, pair_ref, cross_ref)):
        sup = (col % GROUP) ^ j
        out_ref[:, pl.ds(pl.multiple_of(sup * width, width), width)] = ref[...]


def unpack(packed):
    width = packed.shape[-1]
    power = packed[..., width : width + 1, :].astype(jnp.float32)
    return packed[..., :width, :].astype(jnp.float32) * jnp.exp2(power - TOP), power


def add_packed(one, other):
    (a, power_a), (b, power_b) = unpack(one), unpack(other)
    power = jnp.maximum(power_a, power_b) + 1.0
    rows = jnp.broadcast_to(power, (one.shape[0] - one.shape[1], one.shape[1]))
    return jnp.concatenate([(a + b) * jnp.exp2(TOP - power), rows]).astype(one.dtype)


def per_device(anc_inverse, factor_rows, structure, pivot_inverse):
    width = factor_rows.shape[1]
    n_col = lax.axis_size("col")
    all_blocks = factor_rows.shape[0] * n_col
    bf16, f32 = jnp.bfloat16, jnp.float32
    col = lax.axis_index("col")
    row = lax.axis_index("row")
    place = jnp.stack([col, row]).astype(jnp.int32)
    rows = anc_inverse.shape[0]
    half_w = anc_inverse.shape[1] // all_blocks

    def swap(x, flip):
        return lax.ppermute(x, "col", [(c, c ^ flip) for c in range(n_col)])

    def middle(x):
        return lax.ppermute(x, "col", [(c, c ^ 12) for c in range(n_col) if c // 4 in (1, 2)])

    def outward(x):
        return lax.ppermute(x, "col", [(c, c ^ 4) for c in range(n_col) if c // 4 in (1, 2)])

    def across(x):
        return lax.ppermute(x, "row", [(0, 1), (1, 0)])

    first_pair, first_core = col // 2 % 2 == 0, col % 2 == 0

    def choose(x, is_first):
        half = x.shape[1] // 2
        return jnp.where(is_first, x[:, :half], x[:, half:])

    own_rows, place = together((factor_rows.reshape(width, -1), place))
    from_pair = swap(choose(own_rows, ~first_pair), 2)
    pair_rows = choose(own_rows, first_pair)
    part_a = jnp.stack([choose(pair_rows, first_core), swap(choose(pair_rows, ~first_core), 1)])
    inverse = anc_inverse.reshape(rows, half_w, all_blocks).transpose(2, 0, 1)
    two_a = swap(after(part_a, inverse), 8)
    part_b = jnp.stack([choose(from_pair, first_core), swap(choose(from_pair, ~first_core), 1)])

    one_a = swap(after(part_a, inverse), 4)
    x_all, y_all = across(inverse), swap(after(inverse, from_pair), 2)
    own = jnp.concatenate([part_a, part_b])
    n_first = 6 * all_blocks // 16
    c_first = swap(after(inverse[:n_first], two_a, one_a), 1)
    first = together((part_b, inverse[n_first:]), c_first)
    two_b, one_b, c_rest = swap(first[0], 8), swap(first[0], 4), swap(first[1], 1)
    c_own = jnp.concatenate([c_first, c_rest])
    two, one = jnp.concatenate([two_a, two_b]), jnp.concatenate([one_a, one_b])

    n_low = all_blocks // 2
    second = together((two, own, y_all[:n_low], x_all[n_low:], x_all, y_all), one, c_rest)
    out, three = outward(second[0]), middle(second[1])
    xy_low, xy_high = across(second[2]), swap(second[3], 2)
    c_x, c_y = swap(second[4], 1), swap(second[5], 1)

    def product(slots, groups, level, sides, highs=(), sums=None, before=None, ends=True):
        extra = [v for v in (sums, before) if v is not None]
        packs = before is not None
        sel = jax.ShapeDtypeStruct((2, width, width), bf16)
        total = jax.ShapeDtypeStruct((2, width, width), f32)
        diag = jax.ShapeDtypeStruct((width + 16 if packs else width, width), f32)
        arrays = [*level, *sides, *highs, *extra]
        return pl.pallas_call(
            functools.partial(
                product_kernel, slots, len(level), groups, sums is None, ends, packs
            ),
            out_shape=(sel, diag) if ends else total,
            in_specs=[SMEM, SMEM] + [VMEM] * len(arrays),
            out_specs=(VMEM, VMEM) if ends else VMEM,
            compiler_params=PARAMS,
        )(place, structure, *arrays)

    near = [inverse, x_all, c_own, c_x]
    sums = product(range(12), (0, 1), [own, one, two], near, ends=False)
    last = together((three, out, xy_low, xy_high), sums)
    cxy_low, cxy_high = swap(last[2], 1), swap(last[3], 1)
    level = [own, one, two, last[0], last[1]]
    sel_near, diag = product(range(12, 16), (0, 1), level, near, sums=sums)
    s_core = swap(sel_near[1], 1)
    sel_far, diag = product(
        range(16), (2, 3), level, [y_all, xy_low, c_y, cxy_low], [xy_high, cxy_high], before=diag
    )
    s_pair, s_cross = swap(sel_far[0], 2), swap(sel_far[1], 3)

    packed = diag.astype(jnp.float16)
    packed = add_packed(packed, swap(packed, 4))
    packed = add_packed(packed, swap(after(packed, s_core, s_cross), 8))
    selected = pl.pallas_call(
        merge_kernel,
        out_shape=jax.ShapeDtypeStruct((width, GROUP * width), bf16),
        in_specs=[SMEM, VMEM, VMEM, VMEM, VMEM],
        out_specs=VMEM,
        compiler_params=PARAMS,
    )(place, sel_near[0], s_core, s_pair, s_cross)
    got = swap(after(packed, s_pair), 2)
    mine = jnp.stack([jnp.where(first_pair, packed, got), jnp.where(first_pair, got, packed)])
    other = swap(after(mine, selected), 1)
    ordered = [jnp.where(first_core, mine, other), jnp.where(first_core, other, mine)]
    pivots = pivot_inverse.reshape(2, 2, width, width)
    diagonal = jnp.stack([pivots[:, i] - unpack(half)[0] for i, half in enumerate(ordered)], axis=1)
    diagonal = diagonal.reshape(pivot_inverse.shape)
    return selected.reshape(factor_rows.shape), diagonal


def solution(mesh):
    in_specs = (P("col", "row"), P("col", None, "row"), P(), P("row", None, None))
    out_specs = (P("col", None, "row"), P("row", None, None))

    def run(anc_inverse, factor_rows, structure, pivot_inverse):
        n_col, n_row = mesh.shape["col"], mesh.shape["row"]
        blocks, width, columns = factor_rows.shape
        fits = n_col == 16 and n_row == 2 and blocks == n_col and columns == n_row * GROUP * width
        return jax.shard_map(
            per_device if fits else generic,
            mesh=mesh,
            in_specs=in_specs,
            out_specs=out_specs,
            check_vma=False,
        )(anc_inverse, factor_rows, structure, pivot_inverse)

    return run
```

```python
import functools

import jax
import jax.numpy as jnp
from jax import lax
from jax.experimental import pallas as pl
from jax.experimental.pallas import tpu as pltpu
from jax.sharding import PartitionSpec as P

VMEM = pl.BlockSpec(memory_space=pltpu.VMEM)
SMEM = pl.BlockSpec(memory_space=pltpu.SMEM)
PARAMS = pltpu.CompilerParams(vmem_limit_bytes=24 * 1024 * 1024)
TOP = 14.0
GROUP = 4


def after(x, *earlier):
    return lax.optimization_barrier((x, *earlier))[0]


def together(wanted, *earlier):
    return lax.optimization_barrier((*wanted, *earlier))[: len(wanted)]


def generic(anc_inverse, factor_rows, structure, pivot_inverse):
    own_blocks = factor_rows.shape[0]
    width = factor_rows.shape[1]
    local_cols = factor_rows.shape[2]
    local_sups = local_cols // width
    inv_rows = anc_inverse.shape[0]
    all_blocks = own_blocks * lax.axis_size("col")
    col_index = lax.axis_index("col")
    row_index = lax.axis_index("row")
    blocks = col_index * own_blocks + jnp.arange(own_blocks, dtype=jnp.int32)
    list_rows = lax.dynamic_slice_in_dim(structure, row_index * local_sups, local_sups, 0)
    in_struct = jnp.any(list_rows[:, :, None] == blocks[None, None, :], axis=1)
    keep_bf = in_struct.T.astype(jnp.bfloat16)[:, None, :, None]
    keep_float = in_struct.T.astype(jnp.float32)[:, None, :, None]
    masked = (factor_rows.reshape(own_blocks, width, local_sups, width) * keep_bf).reshape(
        factor_rows.shape
    )
    gathered = lax.all_gather(anc_inverse, "row", axis=1, tiled=True)
    full_inverse = gathered.reshape(inv_rows, width, all_blocks)
    product = jnp.einsum(
        "iwb,bwn->in",
        full_inverse,
        lax.all_gather(masked, "col", axis=0, tiled=True),
        preferred_element_type=jnp.float32,
    )
    selected = (-(product.reshape(own_blocks, width, local_sups, width) * keep_float)).astype(
        jnp.bfloat16
    )
    selected = selected.reshape(factor_rows.shape)
    factor_flat = masked.reshape(own_blocks * width, local_sups, width)
    selected_flat = selected.reshape(own_blocks * width, local_sups, width)
    local_terms = jnp.einsum(
        "ikp,ikq->kpq", factor_flat, selected_flat, preferred_element_type=jnp.float32
    )
    summed = lax.psum(local_terms, "col")
    return (selected, pivot_inverse - summed)


def is_member(lists, sup, block):
    found = lists[sup, 0] == block
    for i in range(1, lists.shape[1]):
        found = jnp.logical_or(found, lists[sup, i] == block)
    return found


def product_kernel(groups, n_level, ends, packs, *refs):
    if ends:
        place, refs = refs[0], refs[1:]
    else:
        place, lists, refs = refs[0], refs[1], refs[2:]
    level, refs = refs[:n_level], refs[n_level:]
    sides = []
    for _, _, n_arrays, _ in groups:
        sides.append(refs[:n_arrays])
        refs = refs[n_arrays:]
    col, row = place[0], place[1]
    width = level[0].shape[1]
    half = width // 2
    near = pl.ds(pl.multiple_of(row * half, half), half)
    far = pl.ds(pl.multiple_of((1 - row) * half, half), half)
    totals = [None] * len(groups)
    if any(begun for *_, begun in groups):
        sums_ref, refs = refs[0], refs[1:]
        for g, (*_, begun) in enumerate(groups):
            totals[g] = sums_ref[g] if begun else None
    if packs:
        before_ref, refs = refs[0], refs[1:]

    sup = row * GROUP + col % GROUP

    def is_kept(block):
        return place[2 + block] != 0 if ends else is_member(lists, sup, block)

    def inverse_rows(g, block):
        near_ref, low, *high = sides[g]
        if not high:
            return near_ref[block], low[block]
        n_low = low.shape[0]
        from_high = high[0][jnp.maximum(block - n_low, 0)]
        return near_ref[block], jnp.where(
            block < n_low, low[jnp.minimum(block, n_low - 1)], from_high
        )

    for z in sorted({z for _, steps, *_ in groups for z in steps}):
        blocks = [col ^ (z * GROUP + i) for i in range(GROUP)]
        m = []
        for i, block in enumerate(blocks):
            parts = [level[z][i, rows, :] for rows in (near, far)]
            if z == 3:
                parts = [part + level[4][i, rows, :] for part, rows in zip(parts, (near, far))]
            kept = is_kept(block)
            m += [jnp.where(kept, part, jnp.zeros_like(part)) for part in parts]
        here = [g for g, (_, steps, *_) in enumerate(groups) if z in steps]
        rows = [
            jnp.concatenate([v for block in blocks for v in inverse_rows(g, block)], axis=1)
            for g in here
        ]
        terms = jnp.dot(
            jnp.concatenate(rows, axis=0),
            jnp.concatenate(m, axis=0),
            preferred_element_type=jnp.float32,
        )
        for i, g in enumerate(here):
            term = terms[i * width : (i + 1) * width]
            totals[g] = term if totals[g] is None else totals[g] + term
    if not ends:
        sums_out, place_out = refs
        for g, total in enumerate(totals):
            sums_out[g] = total
        place_out[0], place_out[1] = col, row
        for block in range(place_out.shape[0] - 2):
            place_out[2 + block] = is_kept(block).astype(jnp.int32)
        return
    sel_ref, diag_ref = refs
    diag = before_ref[...] if packs else None
    for g, (group, *_) in enumerate(groups):
        kept = is_kept(col ^ group)
        sel = jnp.where(kept, -totals[g], jnp.zeros_like(totals[g])).astype(jnp.bfloat16)
        sel_ref[g] = sel
        term = lax.dot_general(
            level[0][group], sel, (((0,), (0,)), ((), ())), preferred_element_type=jnp.float32
        )
        diag = term if diag is None else diag + term
    if not packs:
        diag_ref[...] = diag
        return
    largest = jnp.maximum(jnp.max(jnp.abs(diag)), 1e-30)
    power = jnp.ceil(jnp.log2(jnp.full((8, 128), largest, jnp.float32)))
    power = jnp.concatenate([power] * (width // 128), axis=1)
    diag_ref[:width] = diag * jnp.exp2(TOP - power[:1])
    for at in range(width, diag_ref.shape[0], 8):
        diag_ref[at : at + 8] = power


def merge_kernel(place, own_ref, core_ref, pair_ref, cross_ref, out_ref):
    col = place[0]
    width = own_ref.shape[0]
    for j, ref in enumerate((own_ref, core_ref, pair_ref, cross_ref)):
        sup = (col % GROUP) ^ j
        out_ref[:, pl.ds(pl.multiple_of(sup * width, width), width)] = ref[...]


def unpack(packed):
    width = packed.shape[-1]
    power = packed[..., width : width + 1, :].astype(jnp.float32)
    return packed[..., :width, :].astype(jnp.float32) * jnp.exp2(power - TOP), power


def add_packed(one, other):
    (a, power_a), (b, power_b) = unpack(one), unpack(other)
    power = jnp.maximum(power_a, power_b) + 1.0
    rows = jnp.broadcast_to(power, (one.shape[0] - one.shape[1], one.shape[1]))
    return jnp.concatenate([(a + b) * jnp.exp2(TOP - power), rows]).astype(one.dtype)


def per_device(anc_inverse, factor_rows, structure, pivot_inverse):
    width = factor_rows.shape[1]
    n_col = lax.axis_size("col")
    all_blocks = factor_rows.shape[0] * n_col
    bf16, f32 = jnp.bfloat16, jnp.float32
    col = lax.axis_index("col")
    row = lax.axis_index("row")
    place = jnp.stack([col, row]).astype(jnp.int32)
    rows = anc_inverse.shape[0]
    half_w = anc_inverse.shape[1] // all_blocks

    def swap(x, flip):
        return lax.ppermute(x, "col", [(c, c ^ flip) for c in range(n_col)])

    def middle(x):
        return lax.ppermute(x, "col", [(c, c ^ 12) for c in range(n_col) if c // 4 in (1, 2)])

    def outward(x):
        return lax.ppermute(x, "col", [(c, c ^ 4) for c in range(n_col) if c // 4 in (1, 2)])

    def across(x):
        return lax.ppermute(x, "row", [(0, 1), (1, 0)])

    first_pair, first_core = col // 2 % 2 == 0, col % 2 == 0

    def choose(x, is_first):
        half = x.shape[1] // 2
        return jnp.where(is_first, x[:, :half], x[:, half:])

    own_rows, place = together((factor_rows.reshape(width, -1), place))
    from_pair = swap(choose(own_rows, ~first_pair), 2)
    pair_rows = choose(own_rows, first_pair)
    part_a = jnp.stack([choose(pair_rows, first_core), swap(choose(pair_rows, ~first_core), 1)])
    inverse = anc_inverse.reshape(rows, half_w, all_blocks).transpose(2, 0, 1)
    two_a, one_a = swap(after(part_a, inverse), 8), swap(after(part_a, inverse), 4)
    give_b = choose(from_pair, ~first_core)
    part_b = jnp.stack([choose(from_pair, first_core), swap(give_b, 1)])
    x_all, y_all = across(inverse), swap(after(inverse, from_pair), 2)
    own = jnp.concatenate([part_a, part_b])
    n_first = 6 * all_blocks // 16
    c_first = swap(after(inverse[:n_first], two_a, one_a), 1)
    first = together((part_b, inverse[n_first:]), c_first)
    two_b, one_b, c_rest = swap(first[0], 8), swap(first[0], 4), swap(first[1], 1)
    c_own = jnp.concatenate([c_first, c_rest])
    two, one = jnp.concatenate([two_a, two_b]), jnp.concatenate([one_a, one_b])
    n_low = 9 * all_blocks // 16
    second = together((two, own, y_all[:n_low], x_all[n_low:], x_all, y_all), one, c_rest)
    out, three = outward(second[0]), middle(second[1])
    xy_low, xy_high = across(second[2]), swap(second[3], 2)
    c_x, c_y = swap(second[4], 1), swap(second[5], 1)

    def product(scalars, level, groups, sums=None, before=None, ends=True):
        packs = before is not None
        what = tuple((g, tuple(steps), len(v), sums is not None and g < 2) for g, steps, v in groups)
        arrays = [*level, *(v for _, _, arrays in groups for v in arrays)]
        arrays += [v for v in (sums, before) if v is not None]
        sel = jax.ShapeDtypeStruct((len(groups), width, width), bf16)
        total = jax.ShapeDtypeStruct((len(groups), width, width), f32)
        diag = jax.ShapeDtypeStruct((width + 16 if packs else width, width), f32)
        return pl.pallas_call(
            functools.partial(product_kernel, what, len(level), ends, packs),
            out_shape=(sel, diag) if ends else (total, jax.ShapeDtypeStruct((2 + all_blocks,), jnp.int32)),
            in_specs=[SMEM] * len(scalars) + [VMEM] * len(arrays),
            out_specs=(VMEM, VMEM) if ends else (VMEM, SMEM),
            compiler_params=PARAMS,
        )(*scalars, *arrays)

    early, late, steps = (0, 1, 2), (3,), (0, 1, 2, 3)
    rows_0, rows_1 = (inverse, x_all), (c_own, c_x)
    first_groups = [(0, early, rows_0), (1, early, rows_1)]
    sums, kept = product((place, structure), [own, one, two], first_groups, ends=False)
    last = together((three, out, xy_high, xy_low), sums)
    cxy_low, cxy_high = swap(last[3], 1), swap(last[2], 1)
    level = [own, one, two, last[0], last[1]]
    groups = [(0, late, rows_0), (1, late, rows_1), (2, steps, (y_all, last[3], last[2]))]
    sel, diag = product((kept,), level, groups, sums=sums)
    s_core, s_pair = swap(sel[1], 1), swap(sel[2], 2)
    sel_cross, diag = product((kept,), level, [(3, steps, (c_y, cxy_low, cxy_high))], before=diag)
    s_cross = swap(sel_cross[0], 3)

    packed = diag.astype(jnp.float16)
    packed = add_packed(packed, swap(packed, 4))
    packed = add_packed(packed, swap(after(packed, s_core, s_pair), 8))
    selected = pl.pallas_call(
        merge_kernel,
        out_shape=jax.ShapeDtypeStruct((width, GROUP * width), bf16),
        in_specs=[SMEM, VMEM, VMEM, VMEM, VMEM],
        out_specs=VMEM,
        compiler_params=PARAMS,
    )(place, sel[0], s_core, s_pair, s_cross)
    got = swap(after(packed, s_cross), 2)
    mine = jnp.stack([jnp.where(first_pair, packed, got), jnp.where(first_pair, got, packed)])
    other = swap(after(mine, selected), 1)
    ordered = [jnp.where(first_core, mine, other), jnp.where(first_core, other, mine)]
    pivots = pivot_inverse.reshape(2, 2, width, width)
    diagonal = jnp.stack([pivots[:, i] - unpack(half)[0] for i, half in enumerate(ordered)], axis=1)
    diagonal = diagonal.reshape(pivot_inverse.shape)
    return selected.reshape(factor_rows.shape), diagonal


def solution(mesh):
    in_specs = (P("col", "row"), P("col", None, "row"), P(), P("row", None, None))
    out_specs = (P("col", None, "row"), P("row", None, None))

    def run(anc_inverse, factor_rows, structure, pivot_inverse):
        n_col, n_row = mesh.shape["col"], mesh.shape["row"]
        blocks, width, columns = factor_rows.shape
        fits = n_col == 16 and n_row == 2 and blocks == n_col and columns == n_row * GROUP * width
        return jax.shard_map(
            per_device if fits else generic,
            mesh=mesh,
            in_specs=in_specs,
            out_specs=out_specs,
            check_vma=False,
        )(anc_inverse, factor_rows, structure, pivot_inverse)

    return run
```

```python
import functools

import jax
import jax.numpy as jnp
from jax import lax
from jax.experimental import pallas as pl
from jax.experimental.pallas import tpu as pltpu
from jax.sharding import PartitionSpec as P

VMEM = pl.BlockSpec(memory_space=pltpu.VMEM)
SMEM = pl.BlockSpec(memory_space=pltpu.SMEM)
PARAMS = pltpu.CompilerParams(vmem_limit_bytes=24 * 1024 * 1024)
TOP = 14.0
GROUP = 4


def after(x, *earlier):
    return lax.optimization_barrier((x, *earlier))[0]


def together(wanted, *earlier):
    return lax.optimization_barrier((*wanted, *earlier))[: len(wanted)]


def generic(anc_inverse, factor_rows, structure, pivot_inverse):
    own_blocks = factor_rows.shape[0]
    width = factor_rows.shape[1]
    local_cols = factor_rows.shape[2]
    local_sups = local_cols // width
    inv_rows = anc_inverse.shape[0]
    all_blocks = own_blocks * lax.axis_size("col")
    col_index = lax.axis_index("col")
    row_index = lax.axis_index("row")
    blocks = col_index * own_blocks + jnp.arange(own_blocks, dtype=jnp.int32)
    list_rows = lax.dynamic_slice_in_dim(structure, row_index * local_sups, local_sups, 0)
    in_struct = jnp.any(list_rows[:, :, None] == blocks[None, None, :], axis=1)
    keep_bf = in_struct.T.astype(jnp.bfloat16)[:, None, :, None]
    keep_float = in_struct.T.astype(jnp.float32)[:, None, :, None]
    masked = (factor_rows.reshape(own_blocks, width, local_sups, width) * keep_bf).reshape(
        factor_rows.shape
    )
    gathered = lax.all_gather(anc_inverse, "row", axis=1, tiled=True)
    full_inverse = gathered.reshape(inv_rows, width, all_blocks)
    product = jnp.einsum(
        "iwb,bwn->in",
        full_inverse,
        lax.all_gather(masked, "col", axis=0, tiled=True),
        preferred_element_type=jnp.float32,
    )
    selected = (-(product.reshape(own_blocks, width, local_sups, width) * keep_float)).astype(
        jnp.bfloat16
    )
    selected = selected.reshape(factor_rows.shape)
    factor_flat = masked.reshape(own_blocks * width, local_sups, width)
    selected_flat = selected.reshape(own_blocks * width, local_sups, width)
    local_terms = jnp.einsum(
        "ikp,ikq->kpq", factor_flat, selected_flat, preferred_element_type=jnp.float32
    )
    summed = lax.psum(local_terms, "col")
    return (selected, pivot_inverse - summed)


def is_member(lists, sup, block):
    found = lists[sup, 0] == block
    for i in range(1, lists.shape[1]):
        found = jnp.logical_or(found, lists[sup, i] == block)
    return found


def product_kernel(groups, n_level, ends, packs, *refs):
    if ends:
        place, refs = refs[0], refs[1:]
    else:
        place, lists, refs = refs[0], refs[1], refs[2:]
    level, refs = refs[:n_level], refs[n_level:]
    sides = []
    for _, _, n_arrays, _ in groups:
        sides.append(refs[:n_arrays])
        refs = refs[n_arrays:]
    col, row = place[0], place[1]
    width = level[0].shape[1]
    half = width // 2
    near = pl.ds(pl.multiple_of(row * half, half), half)
    far = pl.ds(pl.multiple_of((1 - row) * half, half), half)
    totals = [None] * len(groups)
    if any(begun for *_, begun in groups):
        sums_ref, refs = refs[0], refs[1:]
        for g, (*_, begun) in enumerate(groups):
            totals[g] = sums_ref[g] if begun else None
    if packs:
        before_ref, refs = refs[0], refs[1:]

    sup = row * GROUP + col % GROUP

    def is_kept(block):
        return place[2 + block] != 0 if ends else is_member(lists, sup, block)

    def inverse_rows(g, block):
        near_ref, low, *high = sides[g]
        if not high:
            return near_ref[block], low[block]
        n_low = low.shape[0]
        from_high = high[0][jnp.maximum(block - n_low, 0)]
        return near_ref[block], jnp.where(
            block < n_low, low[jnp.minimum(block, n_low - 1)], from_high
        )

    for z in sorted({z for _, steps, *_ in groups for z in steps}):
        blocks = [col ^ (z * GROUP + i) for i in range(GROUP)]
        m = []
        for i, block in enumerate(blocks):
            parts = [level[z][i, rows, :] for rows in (near, far)]
            if z == 3:
                parts = [part + level[4][i, rows, :] for part, rows in zip(parts, (near, far))]
            kept = is_kept(block)
            m += [jnp.where(kept, part, jnp.zeros_like(part)) for part in parts]
        here = [g for g, (_, steps, *_) in enumerate(groups) if z in steps]
        rows = [
            jnp.concatenate([v for block in blocks for v in inverse_rows(g, block)], axis=1)
            for g in here
        ]
        terms = jnp.dot(
            jnp.concatenate(rows, axis=0),
            jnp.concatenate(m, axis=0),
            preferred_element_type=jnp.float32,
        )
        for i, g in enumerate(here):
            term = terms[i * width : (i + 1) * width]
            totals[g] = term if totals[g] is None else totals[g] + term
    if not ends:
        sums_out, place_out = refs
        for g, total in enumerate(totals):
            sums_out[g] = total
        place_out[0], place_out[1] = col, row
        for block in range(place_out.shape[0] - 2):
            place_out[2 + block] = is_kept(block).astype(jnp.int32)
        return
    sel_ref, diag_ref = refs
    diag = before_ref[...] if packs else None
    for g, (group, *_) in enumerate(groups):
        kept = is_kept(col ^ group)
        sel = jnp.where(kept, -totals[g], jnp.zeros_like(totals[g])).astype(jnp.bfloat16)
        sel_ref[g] = sel
        term = lax.dot_general(
            level[0][group], sel, (((0,), (0,)), ((), ())), preferred_element_type=jnp.float32
        )
        diag = term if diag is None else diag + term
    if not packs:
        diag_ref[...] = diag
        return
    largest = jnp.maximum(jnp.max(jnp.abs(diag)), 1e-30)
    power = jnp.ceil(jnp.log2(jnp.full((8, 128), largest, jnp.float32)))
    power = jnp.concatenate([power] * (width // 128), axis=1)
    diag_ref[:width] = diag * jnp.exp2(TOP - power[:1])
    for at in range(width, diag_ref.shape[0], 8):
        diag_ref[at : at + 8] = power


def merge_kernel(place, own_ref, core_ref, pair_ref, cross_ref, out_ref):
    col = place[0]
    width = own_ref.shape[0]
    for j, ref in enumerate((own_ref, core_ref, pair_ref, cross_ref)):
        sup = (col % GROUP) ^ j
        out_ref[:, pl.ds(pl.multiple_of(sup * width, width), width)] = ref[...]


def unpack(packed):
    width = packed.shape[-1]
    power = packed[..., width : width + 1, :].astype(jnp.float32)
    return packed[..., :width, :].astype(jnp.float32) * jnp.exp2(power - TOP), power


def add_packed(one, other):
    (a, power_a), (b, power_b) = unpack(one), unpack(other)
    power = jnp.maximum(power_a, power_b) + 1.0
    rows = jnp.broadcast_to(power, (one.shape[0] - one.shape[1], one.shape[1]))
    return jnp.concatenate([(a + b) * jnp.exp2(TOP - power), rows]).astype(one.dtype)


def per_device(anc_inverse, factor_rows, structure, pivot_inverse):
    width = factor_rows.shape[1]
    n_col = lax.axis_size("col")
    all_blocks = factor_rows.shape[0] * n_col
    bf16, f32 = jnp.bfloat16, jnp.float32
    col = lax.axis_index("col")
    row = lax.axis_index("row")
    place = jnp.stack([col, row]).astype(jnp.int32)
    rows = anc_inverse.shape[0]
    half_w = anc_inverse.shape[1] // all_blocks

    def swap(x, flip):
        return lax.ppermute(x, "col", [(c, c ^ flip) for c in range(n_col)])

    def middle(x):
        return lax.ppermute(x, "col", [(c, c ^ 12) for c in range(n_col) if c // 4 in (1, 2)])

    def outward(x):
        return lax.ppermute(x, "col", [(c, c ^ 4) for c in range(n_col) if c // 4 in (1, 2)])

    def across(x):
        return lax.ppermute(x, "row", [(0, 1), (1, 0)])

    first_pair, first_core = col // 2 % 2 == 0, col % 2 == 0

    def choose(x, is_first):
        half = x.shape[1] // 2
        return jnp.where(is_first, x[:, :half], x[:, half:])

    own_rows, place = together((factor_rows.reshape(width, -1), place))
    from_pair = swap(choose(own_rows, ~first_pair), 2)
    pair_rows = choose(own_rows, first_pair)
    part_a = jnp.stack([choose(pair_rows, first_core), swap(choose(pair_rows, ~first_core), 1)])
    inverse = anc_inverse.reshape(rows, half_w, all_blocks).transpose(2, 0, 1)
    two_a, one_a = swap(part_a, 8), swap(after(part_a, inverse), 4)
    give_b = choose(from_pair, ~first_core)
    part_b = jnp.stack([choose(from_pair, first_core), swap(give_b, 1)])
    x_all, y_all = across(inverse), swap(after(inverse, from_pair), 2)
    own = jnp.concatenate([part_a, part_b])
    n_first = 7 * all_blocks // 16
    c_first = swap(after(inverse[:n_first], two_a, one_a), 1)
    first = together((part_b, inverse[n_first:]), c_first)
    two_b, one_b, c_rest = swap(first[0], 8), swap(first[0], 4), swap(first[1], 1)
    c_own = jnp.concatenate([c_first, c_rest])
    two, one = jnp.concatenate([two_a, two_b]), jnp.concatenate([one_a, one_b])
    n_low = 7 * all_blocks // 16
    second = together((x_all, y_all, y_all[:n_low], x_all[n_low:], two, own), c_rest, one)
    out, three = outward(second[4]), middle(second[5])
    xy_low, xy_high = across(second[2]), swap(second[3], 2)
    c_x, c_y = swap(second[0], 1), swap(second[1], 1)

    def product(scalars, level, groups, sums=None, before=None, ends=True):
        packs = before is not None
        what = tuple((g, tuple(steps), len(v), sums is not None and g < 2) for g, steps, v in groups)
        arrays = [*level, *(v for _, _, arrays in groups for v in arrays)]
        arrays += [v for v in (sums, before) if v is not None]
        sel = jax.ShapeDtypeStruct((len(groups), width, width), bf16)
        total = jax.ShapeDtypeStruct((len(groups), width, width), f32)
        diag = jax.ShapeDtypeStruct((width + 16 if packs else width, width), f32)
        return pl.pallas_call(
            functools.partial(product_kernel, what, len(level), ends, packs),
            out_shape=(sel, diag) if ends else (total, jax.ShapeDtypeStruct((2 + all_blocks,), jnp.int32)),
            in_specs=[SMEM] * len(scalars) + [VMEM] * len(arrays),
            out_specs=(VMEM, VMEM) if ends else (VMEM, SMEM),
            compiler_params=PARAMS,
        )(*scalars, *arrays)

    early, late, steps = (0, 1, 2), (3,), (0, 1, 2, 3)
    rows_0, rows_1 = (inverse, x_all), (c_own, c_x)
    first_groups = [(0, early, rows_0), (1, early, rows_1)]
    sums, kept = product((place, structure), [own, one, two], first_groups, ends=False)
    last = together((three, out, xy_low, xy_high), sums)
    cxy_low, cxy_high = swap(last[2], 1), swap(last[3], 1)
    level = [own, one, two, last[0], last[1]]
    groups = [(0, late, rows_0), (1, late, rows_1), (2, steps, (y_all, last[2], last[3]))]
    sel, diag = product((kept,), level, groups, sums=sums)
    s_core, s_pair = swap(sel[1], 1), swap(sel[2], 2)
    sel_cross, diag = product((kept,), level, [(3, steps, (c_y, cxy_low, cxy_high))], before=diag)
    s_cross = swap(sel_cross[0], 3)

    packed = diag.astype(jnp.float16)
    packed = add_packed(packed, swap(packed, 4))
    packed = add_packed(packed, swap(after(packed, s_core, s_pair), 8))
    selected = pl.pallas_call(
        merge_kernel,
        out_shape=jax.ShapeDtypeStruct((width, GROUP * width), bf16),
        in_specs=[SMEM, VMEM, VMEM, VMEM, VMEM],
        out_specs=VMEM,
        compiler_params=PARAMS,
    )(place, sel[0], s_core, s_pair, s_cross)
    got = swap(after(packed, s_cross), 2)
    mine = jnp.stack([jnp.where(first_pair, packed, got), jnp.where(first_pair, got, packed)])
    other = swap(after(mine, selected), 1)
    ordered = [jnp.where(first_core, mine, other), jnp.where(first_core, other, mine)]
    pivots = pivot_inverse.reshape(2, 2, width, width)
    diagonal = jnp.stack([pivots[:, i] - unpack(half)[0] for i, half in enumerate(ordered)], axis=1)
    diagonal = diagonal.reshape(pivot_inverse.shape)
    return selected.reshape(factor_rows.shape), diagonal


def solution(mesh):
    in_specs = (P("col", "row"), P("col", None, "row"), P(), P("row", None, None))
    out_specs = (P("col", None, "row"), P("row", None, None))

    def run(anc_inverse, factor_rows, structure, pivot_inverse):
        n_col, n_row = mesh.shape["col"], mesh.shape["row"]
        blocks, width, columns = factor_rows.shape
        fits = n_col == 16 and n_row == 2 and blocks == n_col and columns == n_row * GROUP * width
        return jax.shard_map(
            per_device if fits else generic,
            mesh=mesh,
            in_specs=in_specs,
            out_specs=out_specs,
            check_vma=False,
        )(anc_inverse, factor_rows, structure, pivot_inverse)

    return run
```
